512 devices in a mesh: tm: 32 (over z, x_lo, core), space: 16 (over y, x_hi).
Axes of the slice: x: 4 (x_hi: 2, x_lo: 2; x = x_hi * 2 + x_lo), y: 8, z: 8, core: 2. Of those that a mesh axis runs over, the one named last changes fastest.
Arguments:
- snapshots: bfloat16 [16384, 49152], P('tm', 'space')
- freq_ids: int32 [64], replicated, may hold values from 0 to 127
Outputs:
- gram: float32 [64, 2, 63, 63], P('tm')
The draws below stay inside these ranges and needn't reach their ends.
All inputs are finite; a program needn't handle non-finite values.
Results may differ from the reference program's by a relative error of at most 0.00039.
Values may be sent and summed in bfloat16 or wider, within the bound.
A program may use at most 64 MiB of HBM per device.

```python
import math
import jax
import jax.numpy as jnp
from jax import lax

NFFT = 512
F = 64
NB = 63
TIMES = 16384
PTS = 49152


def draw_snapshots(key, part):
    keys = jax.random.split(key, 5)
    noise = jax.random.normal(keys[0], (TIMES, PTS), jnp.float32)
    scales = jnp.exp(jax.random.uniform(keys[1], (PTS,), jnp.float32, math.log(0.5), math.log(2.0)))
    times = jnp.arange(TIMES, dtype=jnp.float32)
    bins = jax.random.uniform(keys[2], (12,), jnp.float32, 0.0, NFFT / 4.0)
    omegas = bins * (2.0 * math.pi / NFFT)
    amp_cos = 0.15 * jax.random.normal(keys[3], (12, PTS), jnp.float32)
    sine_amplitude = 0.15 * jax.random.normal(keys[4], (12, PTS), jnp.float32)
    field = noise
    for index in range(12):
        phase = omegas[index] * times
        field = field + jnp.cos(phase)[:, None] * amp_cos[index][None, :] + jnp.sin(phase)[:, None] * sine_amplitude[index][None, :]
    return (field * scales[None, :]).astype(jnp.bfloat16)


def touch_ends(drawn, stream_key, low, largest):
    extent = drawn.shape
    place = [jax.random.randint(jax.random.fold_in(stream_key, axis), (), 0, extent[axis]) for axis in range(len(extent))]
    drawn = drawn.at[tuple(place)].set(low)
    longest = extent.index(max(extent))
    place[longest] = (place[longest] + 1) % extent[longest]
    return drawn.at[tuple(place)].set(largest)


def setup_inputs(seed: int = 0) -> dict:
    streams_of = jax.random.split(jax.random.key(seed), 3)
    return {
        "snapshots": draw_snapshots(jax.random.fold_in(streams_of[2], 71), 0),
        "freq_ids": touch_ends(jax.random.randint(streams_of[1], (F,), 0, NFFT // 4), jax.random.fold_in(streams_of[1], 1), 0, (NFFT // 4) - 1).astype(jnp.int32),
    }


def kernel_values(freqs, shifts, window_length):
    phase = (freqs * shifts) % window_length
    angle = (2.0 * math.pi / window_length) * phase.astype(jnp.float32)
    window = 0.5 - 0.5 * jnp.cos((2.0 * math.pi / window_length) * shifts.astype(jnp.float32))
    return window * jnp.cos(angle), -window * jnp.sin(angle)


def reference(snapshots, freq_ids):
    shifts = jnp.arange(NFFT, dtype=jnp.int32)
    real_part, imag_part = kernel_values(freq_ids[:, None], shifts[None, :], NFFT)
    table = jnp.stack([real_part, imag_part], axis=1).reshape(2 * F, NFFT).astype(jnp.bfloat16)
    starts = (jnp.arange(NB, dtype=jnp.int32) * (NFFT // 2)).astype(jnp.int32)

    def one_block(start):
        segment = lax.dynamic_slice_in_dim(snapshots, start, NFFT, 0)
        return jnp.dot(table, segment, preferred_element_type=jnp.float32).astype(jnp.bfloat16)

    blockdft = lax.map(one_block, starts)
    scale = 1.0 / (NFFT * PTS)

    def one_freq(index):
        pair = lax.dynamic_slice_in_dim(blockdft, (2 * index).astype(jnp.int32), 2, 1)
        stacked_snapshot_rows = jnp.concatenate([pair[:, 0, :], pair[:, 1, :]], axis=0)
        cross_product_terms = jnp.dot(stacked_snapshot_rows, stacked_snapshot_rows.T, preferred_element_type=jnp.float32)
        gram_real_matrix = cross_product_terms[:NB, :NB] + cross_product_terms[NB:, NB:]
        imag_gram = cross_product_terms[NB:, :NB] - cross_product_terms[:NB, NB:]
        return jnp.stack([gram_real_matrix, imag_gram], axis=0) * scale

    return lax.map(one_freq, jnp.arange(F, dtype=jnp.int32))
```

```python
import functools
import math

import jax
import jax.numpy as jnp
from jax import lax
from jax.experimental import pallas as pl
from jax.experimental.pallas import tpu as pltpu
from jax.sharding import PartitionSpec as P

NFFT = 512
HALF = NFFT // 2
MESH = pl.DeviceIdType.MESH
F32 = jnp.float32
BF16 = jnp.bfloat16

ROWS = 16
PARTS = 3


def cosine(m):
    b = jnp.abs(m - 256) - 128
    x = b.astype(F32) * (2.0 * math.pi / NFFT)
    s = x * x
    p = jnp.full_like(x, 1.0 / math.factorial(13))
    for k in (11, 9, 7, 5, 3, 1):
        p = p * s + (-1.0 if k % 4 == 3 else 1.0) / math.factorial(k)
    return x * p


def iota(shape, dim):
    return lax.broadcasted_iota(jnp.int32, shape, dim)


def basis(freqs, first, n_tm):
    rows = 8 * n_tm
    row = iota((rows, freqs.shape[1]), 0)
    column = iota((rows, freqs.shape[1]), 1)
    wanted = 2 * lax.rem(first + row // 8, n_tm) + (row // 2) % 2
    freq = jnp.sum(jnp.where(column == wanted, freqs, 0).astype(F32), axis=1, keepdims=True)
    freq = freq.astype(jnp.int32)
    row = iota((rows, 1), 0)
    phase = freq * iota((rows, HALF), 1) + 128 * (row % 2)
    return cosine(phase & (NFFT - 1)), 1.0 - 2.0 * (freq & 1).astype(F32), (row // 4) % 2


def kernel(
    n_tm, n_space, lanes, scale,
    freq_ref, x_hbm, out_ref,
    x, even_w, left_w, right_w, swap,
    even, give_left, give_right, keep_left, keep_right, got_left, got_right, odd_left, odd_right,
    recv, gram, mine, shares, total,
    x_sem, give_sem, got_sem, send_sem, recv_sem, space_send, space_recv,
):
    me = lax.axis_index("tm")
    spot = lax.axis_index("space")
    blocks = 2 * n_tm
    half = n_tm // 2
    width = 4 * lanes

    barrier = pltpu.get_barrier_semaphore()

    @pl.loop(1, n_tm)
    def _(r):
        pl.semaphore_signal(
            barrier, inc=1, device_id={"tm": lax.rem(me + r, n_tm)}, device_id_type=MESH
        )

    @pl.loop(1, n_space)
    def _(r):
        pl.semaphore_signal(
            barrier, inc=1, device_id={"space": lax.rem(spot + r, n_space)}, device_id_type=MESH
        )

    def load(part):
        columns = pl.ds(pl.multiple_of(part * width, width), width)
        return pltpu.make_async_copy(x_hbm.at[:, columns], x.at[part], x_sem.at[part])

    for part in range(PARTS):
        load(part).start()

    window = 0.5 * cosine(iota((1, HALF), 1))
    rising, falling = 0.5 - window, 0.5 + window
    freqs = freq_ref[...]
    wave, sign, which = basis(freqs, me, n_tm)
    for h in range(2):
        kept = (which == h).astype(F32)
        even_w[h, :, :HALF] = (wave * rising * kept).astype(BF16)
        late = (wave * falling * (sign * kept)).astype(BF16)
        even_w[h, :, HALF:] = late
        left_w[h] = late
    wave, sign, which = basis(freqs, me + 1, n_tm)
    for h in range(2):
        right_w[h] = (wave * rising * (which == h).astype(F32)).astype(BF16)

    side = ROWS * ROWS
    out_row, in_row = iota((side, side), 0), iota((side, side), 1)
    swap[...] = (in_row == (out_row % ROWS) * ROWS + out_row // ROWS).astype(F32).astype(BF16)

    def transform(part, weights, start, stop):
        halves = []
        for pair in range(2):
            acc = None
            for h in range(2):
                columns = slice((2 * pair + h) * lanes, (2 * pair + h + 1) * lanes)
                term = jnp.dot(
                    weights[h], x[part, start:stop, columns], preferred_element_type=F32
                )
                acc = term if acc is None else acc + term
            halves.append(acc.reshape(n_tm, 8, lanes))
        return jnp.concatenate(halves, axis=1)

    def to_right(part):
        return pltpu.make_async_remote_copy(
            src_ref=give_right.at[part], dst_ref=got_left.at[part],
            send_sem=give_sem.at[0, part], recv_sem=got_sem.at[0, part],
            device_id={"tm": lax.rem(me + 1, n_tm)}, device_id_type=MESH,
        )

    def to_left(part):
        return pltpu.make_async_remote_copy(
            src_ref=give_left.at[part], dst_ref=got_right.at[part],
            send_sem=give_sem.at[1, part], recv_sem=got_sem.at[1, part],
            device_id={"tm": lax.rem(me + n_tm - 1, n_tm)}, device_id_type=MESH,
        )

    def post(part, tile, block, r):
        pltpu.make_async_remote_copy(
            src_ref=tile, dst_ref=recv.at[part, block],
            send_sem=send_sem.at[part], recv_sem=recv_sem.at[part],
            device_id={"tm": lax.rem(me + r, n_tm)}, device_id_type=MESH,
        ).start()

    def place(part, tile, block):
        pltpu.make_async_copy(tile, recv.at[part, block], recv_sem.at[part]).start()

    after = 2 * me + 1
    before = lax.rem(2 * me + blocks - 1, blocks)

    @pl.loop(0, PARTS)
    def _(part):
        load(part).wait()
        partial = transform(part, left_w, 0, HALF)
        keep_left[part] = partial[:half]
        give_left[part] = partial[half:].astype(BF16)
        partial = transform(part, right_w, HALF, NFFT)
        give_right[part] = partial[:half].astype(BF16)
        keep_right[part] = partial[half:]

        @pl.when(part == 0)
        def _():
            pl.semaphore_wait(barrier, n_tm + n_space - 2)

        to_right(part).start()
        to_left(part).start()
        even[part] = transform(part, even_w, 0, NFFT).astype(BF16)
        place(part, even.at[part, 0], 2 * me)
        post(part, even.at[part, half], 2 * me, half)

        @pl.loop(1, half)
        def _(r):
            post(part, even.at[part, r], 2 * me, r)
            post(part, even.at[part, n_tm - r], 2 * me, n_tm - r)

    @pl.loop(0, PARTS)
    def _(part):
        to_right(part).wait_recv()
        odd_left[part] = (keep_left[part] + got_left[part].astype(F32)).astype(BF16)
        to_left(part).wait_recv()
        odd_right[part] = (keep_right[part] + got_right[part].astype(F32)).astype(BF16)
        place(part, odd_left.at[part, 0], before)
        place(part, odd_right.at[part, half - 1], after)

        @pl.loop(1, half)
        def _(r):
            post(part, odd_left.at[part, r], before, r)
            post(part, odd_right.at[part, half - 1 - r], after, n_tm - r)

    gram[...] = jnp.zeros_like(gram)

    @pl.loop(0, PARTS)
    def _(part):
        pltpu.make_async_copy(recv.at[part], recv.at[part], recv_sem.at[part]).wait()
        groups = []
        for g in range(blocks // ROWS):
            tiles = recv[part, g * ROWS : (g + 1) * ROWS].reshape(side, lanes)
            groups.append(jnp.dot(swap[...], tiles, preferred_element_type=F32).astype(BF16))
        for f in range(2):
            acc = gram[f]
            for q in range(4):
                rows = [
                    group[(4 * q + 2 * f + c) * ROWS : (4 * q + 2 * f + c + 1) * ROWS]
                    for c in range(2)
                    for group in groups
                ]
                rows = jnp.concatenate(rows, axis=0)
                acc = acc + lax.dot_general(
                    rows, rows, (((1,), (1,)), ((), ())), preferred_element_type=F32
                )
            gram[f] = acc

    for f in range(2):
        both = gram[f]
        top, bottom = both[:blocks], both[blocks:]
        real_side = iota(top.shape, 1) < blocks
        mine[f * blocks : (f + 1) * blocks, :] = jnp.where(real_side, top, -top) + jnp.concatenate(
            [bottom[:, blocks:], bottom[:, :blocks]], axis=1
        )

    share = 2 * blocks // n_space

    def rows_of(spot):
        return pl.ds(pl.multiple_of(spot * share, share), share)

    @pl.loop(1, n_space)
    def _(r):
        other = lax.rem(spot + r, n_space)
        pltpu.make_async_remote_copy(
            src_ref=mine.at[rows_of(other)], dst_ref=shares.at[spot],
            send_sem=space_send.at[0], recv_sem=space_recv.at[0],
            device_id={"space": other}, device_id_type=MESH,
        ).start()

    shares[spot] = mine[rows_of(spot), :]
    others = shares.at[pl.ds(0, n_space - 1)]
    pltpu.make_async_copy(others, others, space_recv.at[0]).wait()
    total[rows_of(spot), :] = jnp.sum(shares[...], axis=0) * scale

    @pl.loop(1, n_space)
    def _(r):
        pltpu.make_async_remote_copy(
            src_ref=total.at[rows_of(spot)], dst_ref=total.at[rows_of(spot)],
            send_sem=space_send.at[1], recv_sem=space_recv.at[1],
            device_id={"space": lax.rem(spot + r, n_space)}, device_id_type=MESH,
        ).start()

    for part in range(PARTS):
        to_right(part).wait_send()
        to_left(part).wait_send()
        sent = recv.at[part, pl.ds(0, blocks - 3)]
        pltpu.make_async_copy(sent, sent, send_sem.at[part]).wait()
    pltpu.make_async_copy(others, others, space_send.at[0]).wait()
    pltpu.make_async_copy(others, others, space_recv.at[1]).wait()
    out_ref[...] = total[...]
    pltpu.make_async_copy(others, others, space_send.at[1]).wait()


def local(snapshots, freq_ids):
    n_tm, n_space = lax.axis_size("tm"), lax.axis_size("space")
    points = snapshots.shape[1]
    lanes = points // (4 * PARTS)
    blocks, half, rows = 2 * n_tm, n_tm // 2, 8 * n_tm
    dma = pltpu.SemaphoreType.DMA
    out = pl.pallas_call(
        functools.partial(kernel, n_tm, n_space, lanes, 1.0 / (NFFT * points * n_space)),
        out_shape=jax.ShapeDtypeStruct((2 * blocks, 2 * blocks), F32),
        in_specs=[
            pl.BlockSpec(memory_space=pltpu.VMEM),
            pl.BlockSpec(memory_space=pl.ANY),
        ],
        out_specs=pl.BlockSpec(memory_space=pltpu.VMEM),
        scratch_shapes=[
            pltpu.VMEM((PARTS, NFFT, 4 * lanes), BF16),
            pltpu.VMEM((2, rows, NFFT), BF16),
            pltpu.VMEM((2, rows, HALF), BF16),
            pltpu.VMEM((2, rows, HALF), BF16),
            pltpu.VMEM((ROWS * ROWS, ROWS * ROWS), BF16),
            pltpu.VMEM((PARTS, n_tm, ROWS, lanes), BF16),
            pltpu.VMEM((PARTS, half, ROWS, lanes), BF16),
            pltpu.VMEM((PARTS, half, ROWS, lanes), BF16),
            pltpu.VMEM((PARTS, half, ROWS, lanes), F32),
            pltpu.VMEM((PARTS, half, ROWS, lanes), F32),
            pltpu.VMEM((PARTS, half, ROWS, lanes), BF16),
            pltpu.VMEM((PARTS, half, ROWS, lanes), BF16),
            pltpu.VMEM((PARTS, half, ROWS, lanes), BF16),
            pltpu.VMEM((PARTS, half, ROWS, lanes), BF16),
            pltpu.VMEM((PARTS, blocks, ROWS, lanes), BF16),
            pltpu.VMEM((2, 2 * blocks, 2 * blocks), F32),
            pltpu.VMEM((2 * blocks, 2 * blocks), F32),
            pltpu.VMEM((n_space, 2 * blocks // n_space, 2 * blocks), F32),
            pltpu.VMEM((2 * blocks, 2 * blocks), F32),
            dma((PARTS,)),
            dma((2, PARTS)),
            dma((2, PARTS)),
            dma((PARTS,)),
            dma((PARTS,)),
            dma((2,)),
            dma((2,)),
        ],
        compiler_params=pltpu.CompilerParams(
            collective_id=0, has_side_effects=True, vmem_limit_bytes=60 * 2**20
        ),
        name="spod",
    )(freq_ids.reshape(1, -1), snapshots)
    out = out.reshape(2, blocks, 2, blocks).transpose(0, 2, 1, 3)
    return out[:, :, : blocks - 1, : blocks - 1]


def solution(mesh):
    return jax.shard_map(
        local,
        mesh=mesh,
        in_specs=(P("tm", "space"), P()),
        out_specs=P("tm", None, None, None),
        check_vma=False,
    )
```

```python
import functools
import math

import jax
import jax.numpy as jnp
from jax import lax
from jax.experimental import pallas as pl
from jax.experimental.pallas import tpu as pltpu
from jax.sharding import PartitionSpec as P

NFFT = 512
HALF = NFFT // 2
MESH = pl.DeviceIdType.MESH
F32 = jnp.float32
BF16 = jnp.bfloat16

ROWS = 16
PARTS = 3


def cosine(m):
    b = jnp.abs(m - 256) - 128
    x = b.astype(F32) * (2.0 * math.pi / NFFT)
    s = x * x
    p = jnp.full_like(x, 1.0 / math.factorial(13))
    for k in (11, 9, 7, 5, 3, 1):
        p = p * s + (-1.0 if k % 4 == 3 else 1.0) / math.factorial(k)
    return x * p


def iota(shape, dim):
    return lax.broadcasted_iota(jnp.int32, shape, dim)


def basis(freqs, first, n_tm):
    rows = 8 * n_tm
    row = iota((rows, freqs.shape[1]), 0)
    column = iota((rows, freqs.shape[1]), 1)
    wanted = 2 * lax.rem(first + row // 8, n_tm) + (row // 2) % 2
    freq = jnp.sum(jnp.where(column == wanted, freqs, 0).astype(F32), axis=1, keepdims=True)
    freq = freq.astype(jnp.int32)
    row = iota((rows, 1), 0)
    phase = freq * iota((rows, HALF), 1) + 128 * (row % 2)
    return cosine(phase & (NFFT - 1)), 1.0 - 2.0 * (freq & 1).astype(F32), (row // 4) % 2


def far_first(k, n):
    return n // 2 + jnp.where(k % 2 == 0, k // 2, -(k // 2))


def kernel(
    n_tm, n_space, lanes, scale,
    freq_hbm, x_hbm, out_ref,
    freq, x, even_w, left_w, right_w, swap,
    even, give_left, give_right, keep_left, keep_right, got_left, got_right, odd,
    recv, gram, mine, shares, total,
    freq_sem, x_sem, give_sem, got_sem, send_sem, recv_sem, space_send, space_recv,
):
    me = lax.axis_index("tm")
    spot = lax.axis_index("space")
    blocks = 2 * n_tm
    half = n_tm // 2
    width = 4 * lanes

    barrier = pltpu.get_barrier_semaphore()

    @pl.loop(1, n_tm)
    def _(k):
        other = lax.rem(me + far_first(k, n_tm), n_tm)
        pl.semaphore_signal(barrier, inc=1, device_id={"tm": other}, device_id_type=MESH)

    @pl.loop(1, n_space)
    def _(k):
        other = lax.rem(spot + far_first(k, n_space), n_space)
        pl.semaphore_signal(barrier, inc=1, device_id={"space": other}, device_id_type=MESH)

    def load(part):
        columns = pl.ds(pl.multiple_of(part * width, width), width)
        return pltpu.make_async_copy(x_hbm.at[:, columns], x.at[part], x_sem.at[part])

    load_freq = pltpu.make_async_copy(freq_hbm, freq, freq_sem.at[0])
    load_freq.start()
    for part in range(PARTS):
        load(part).start()

    window = 0.5 * cosine(iota((1, HALF), 1))
    rising, falling = 0.5 - window, 0.5 + window
    load_freq.wait()
    freqs = freq[...]
    wave, sign, which = basis(freqs, me, n_tm)
    for h in range(2):
        kept = (which == h).astype(F32)
        even_w[h, :, :HALF] = (wave * rising * kept).astype(BF16)
        late = (wave * falling * (sign * kept)).astype(BF16)
        even_w[h, :, HALF:] = late
        left_w[h] = late
    wave, sign, which = basis(freqs, me + 1, n_tm)
    for h in range(2):
        right_w[h] = (wave * rising * (which == h).astype(F32)).astype(BF16)

    side = ROWS * ROWS
    out_row, in_row = iota((side, side), 0), iota((side, side), 1)
    swap[...] = (in_row == (out_row % ROWS) * ROWS + out_row // ROWS).astype(F32).astype(BF16)

    def transform(part, weights, start, stop):
        halves = []
        for pair in range(2):
            acc = None
            for h in range(2):
                columns = slice((2 * pair + h) * lanes, (2 * pair + h + 1) * lanes)
                term = jnp.dot(
                    weights[h], x[part, start:stop, columns], preferred_element_type=F32
                )
                acc = term if acc is None else acc + term
            halves.append(acc.reshape(n_tm, 8, lanes))
        return jnp.concatenate(halves, axis=1)

    def to_right(part):
        return pltpu.make_async_remote_copy(
            src_ref=give_right.at[part], dst_ref=got_left.at[part],
            send_sem=give_sem.at[0, part], recv_sem=got_sem.at[0, part],
            device_id={"tm": lax.rem(me + 1, n_tm)}, device_id_type=MESH,
        )

    def to_left(part):
        return pltpu.make_async_remote_copy(
            src_ref=give_left.at[part], dst_ref=got_right.at[part],
            send_sem=give_sem.at[1, part], recv_sem=got_sem.at[1, part],
            device_id={"tm": lax.rem(me + n_tm - 1, n_tm)}, device_id_type=MESH,
        )

    def post(part, tile, block, r):
        pltpu.make_async_remote_copy(
            src_ref=tile, dst_ref=recv.at[part, block],
            send_sem=send_sem.at[part], recv_sem=recv_sem.at[part],
            device_id={"tm": lax.rem(me + r, n_tm)}, device_id_type=MESH,
        ).start()

    def place(part, tile, block):
        pltpu.make_async_copy(tile, recv.at[part, block], recv_sem.at[part]).start()

    has_before, has_after = me > 0, me < n_tm - 1
    zeros = jnp.zeros((ROWS, lanes), BF16)
    for part in range(PARTS):
        recv[part, blocks - 1] = zeros

    after = 2 * me + 1
    before = 2 * me - 1

    @pl.loop(0, PARTS)
    def _(part):
        load(part).wait()
        partial = transform(part, left_w, 0, HALF)
        keep_left[part] = partial[:half]
        give_left[part] = partial[half:].astype(BF16)
        partial = transform(part, right_w, HALF, NFFT)
        give_right[part] = partial[:half].astype(BF16)
        keep_right[part] = partial[half:]

        @pl.when(part == 0)
        def _():
            pl.semaphore_wait(barrier, n_tm + n_space - 2)


        @pl.when(has_after)
        def _():
            to_right(part).start()

        @pl.when(has_before)
        def _():
            to_left(part).start()

        even[part] = transform(part, even_w, 0, NFFT).astype(BF16)
        place(part, even.at[part, 0], 2 * me)

        @pl.loop(0, n_tm)
        def _(k):
            r = lax.rem(k + n_tm - me, n_tm)

            @pl.when(r != 0)
            def _():
                post(part, even.at[part, r], 2 * me, r)

    @pl.loop(0, PARTS)
    def _(part):
        @pl.when(has_before)
        def _():
            to_right(part).wait_recv()
            odd[part, :half] = (keep_left[part] + got_left[part].astype(F32)).astype(BF16)
            place(part, odd.at[part, 0], before)

        @pl.when(has_after)
        def _():
            to_left(part).wait_recv()
            summed = (keep_right[part] + got_right[part].astype(F32)).astype(BF16)
            odd[part, half + 1 :] = summed[: half - 1]
            odd[part, half] = summed[half - 1]
            place(part, odd.at[part, half], after)

        @pl.loop(0, n_tm)
        def _(k):
            r = lax.rem(k + n_tm - me, n_tm)

            @pl.when((r > 0) & (r < half) & has_before)
            def _():
                post(part, odd.at[part, r], before, r)

            @pl.when((r > half) & has_after)
            def _():
                post(part, odd.at[part, r], after, r)

    gram[...] = jnp.zeros_like(gram)

    @pl.loop(0, PARTS)
    def _(part):
        arrived = recv.at[part, pl.ds(0, blocks - 1)]
        pltpu.make_async_copy(arrived, arrived, recv_sem.at[part]).wait()
        groups = []
        for g in range(blocks // ROWS):
            tiles = recv[part, g * ROWS : (g + 1) * ROWS].reshape(side, lanes)
            groups.append(jnp.dot(swap[...], tiles, preferred_element_type=F32).astype(BF16))
        for f in range(2):
            acc = gram[f]
            for q in range(4):
                rows = [
                    group[(4 * q + 2 * f + c) * ROWS : (4 * q + 2 * f + c + 1) * ROWS]
                    for c in range(2)
                    for group in groups
                ]
                rows = jnp.concatenate(rows, axis=0)
                acc = acc + lax.dot_general(
                    rows, rows, (((1,), (1,)), ((), ())), preferred_element_type=F32
                )
            gram[f] = acc

    for f in range(2):
        both = gram[f]
        top, bottom = both[:blocks], both[blocks:]
        real_side = iota(top.shape, 1) < blocks
        mine[f * blocks : (f + 1) * blocks, :] = jnp.where(real_side, top, -top) + jnp.concatenate(
            [bottom[:, blocks:], bottom[:, :blocks]], axis=1
        )

    share = 2 * blocks // n_space

    def rows_of(spot):
        return pl.ds(pl.multiple_of(spot * share, share), share)

    @pl.loop(1, n_space)
    def _(k):
        other = lax.rem(spot + far_first(k, n_space), n_space)
        pltpu.make_async_remote_copy(
            src_ref=mine.at[rows_of(other)], dst_ref=shares.at[spot],
            send_sem=space_send.at[0], recv_sem=space_recv.at[0],
            device_id={"space": other}, device_id_type=MESH,
        ).start()

    shares[spot] = mine[rows_of(spot), :]
    others = shares.at[pl.ds(0, n_space - 1)]
    pltpu.make_async_copy(others, others, space_recv.at[0]).wait()
    total[rows_of(spot), :] = jnp.sum(shares[...], axis=0) * scale

    @pl.loop(1, n_space)
    def _(k):
        other = lax.rem(spot + far_first(k, n_space), n_space)
        pltpu.make_async_remote_copy(
            src_ref=total.at[rows_of(spot)], dst_ref=total.at[rows_of(spot)],
            send_sem=space_send.at[1], recv_sem=space_recv.at[1],
            device_id={"space": other}, device_id_type=MESH,
        ).start()

    for part in range(PARTS):
        sent = recv.at[part, pl.ds(0, n_tm - 1)]
        pltpu.make_async_copy(sent, sent, send_sem.at[part]).wait()
        sent = recv.at[part, pl.ds(0, half - 1)]

        @pl.when(has_after)
        def _():
            to_right(part).wait_send()
            pltpu.make_async_copy(sent, sent, send_sem.at[part]).wait()

        @pl.when(has_before)
        def _():
            to_left(part).wait_send()
            pltpu.make_async_copy(sent, sent, send_sem.at[part]).wait()

    pltpu.make_async_copy(others, others, space_send.at[0]).wait()
    pltpu.make_async_copy(others, others, space_recv.at[1]).wait()
    for f in range(2):
        rows = total[f * blocks : (f + 1) * blocks, :]
        out_ref[f, :, 0, :] = rows[: blocks - 1, : blocks - 1]
        out_ref[f, :, 1, :] = rows[: blocks - 1, blocks : 2 * blocks - 1]
    pltpu.make_async_copy(others, others, space_send.at[1]).wait()


def local(snapshots, freq_ids):
    n_tm, n_space = lax.axis_size("tm"), lax.axis_size("space")
    points = snapshots.shape[1]
    lanes = points // (4 * PARTS)
    blocks, half, rows = 2 * n_tm, n_tm // 2, 8 * n_tm
    dma = pltpu.SemaphoreType.DMA
    out = pl.pallas_call(
        functools.partial(kernel, n_tm, n_space, lanes, 1.0 / (NFFT * points * n_space)),
        out_shape=jax.ShapeDtypeStruct((2, blocks - 1, 2, blocks - 1), F32),
        in_specs=[
            pl.BlockSpec(memory_space=pl.ANY),
            pl.BlockSpec(memory_space=pl.ANY),
        ],
        out_specs=pl.BlockSpec(memory_space=pltpu.VMEM),
        scratch_shapes=[
            pltpu.VMEM((1, freq_ids.shape[0]), jnp.int32),
            pltpu.VMEM((PARTS, NFFT, 4 * lanes), BF16),
            pltpu.VMEM((2, rows, NFFT), BF16),
            pltpu.VMEM((2, rows, HALF), BF16),
            pltpu.VMEM((2, rows, HALF), BF16),
            pltpu.VMEM((ROWS * ROWS, ROWS * ROWS), BF16),
            pltpu.VMEM((PARTS, n_tm, ROWS, lanes), BF16),
            pltpu.VMEM((PARTS, half, ROWS, lanes), BF16),
            pltpu.VMEM((PARTS, half, ROWS, lanes), BF16),
            pltpu.VMEM((PARTS, half, ROWS, lanes), F32),
            pltpu.VMEM((PARTS, half, ROWS, lanes), F32),
            pltpu.VMEM((PARTS, half, ROWS, lanes), BF16),
            pltpu.VMEM((PARTS, half, ROWS, lanes), BF16),
            pltpu.VMEM((PARTS, n_tm, ROWS, lanes), BF16),
            pltpu.VMEM((PARTS, blocks, ROWS, lanes), BF16),
            pltpu.VMEM((2, 2 * blocks, 2 * blocks), F32),
            pltpu.VMEM((2 * blocks, 2 * blocks), F32),
            pltpu.VMEM((n_space, 2 * blocks // n_space, 2 * blocks), F32),
            pltpu.VMEM((2 * blocks, 2 * blocks), F32),
            dma((1,)),
            dma((PARTS,)),
            dma((2, PARTS)),
            dma((2, PARTS)),
            dma((PARTS,)),
            dma((PARTS,)),
            dma((2,)),
            dma((2,)),
        ],
        compiler_params=pltpu.CompilerParams(
            collective_id=0, has_side_effects=True, vmem_limit_bytes=48 * 2**20
        ),
        name="spod",
    )(
        pltpu.with_memory_space_constraint(freq_ids.reshape(1, -1), pltpu.HBM),
        pltpu.with_memory_space_constraint(snapshots, pltpu.HBM),
    )
    return out.transpose(0, 2, 1, 3)


def solution(mesh):
    return jax.shard_map(
        local,
        mesh=mesh,
        in_specs=(P("tm", "space"), P()),
        out_specs=P("tm", None, None, None),
        check_vma=False,
    )
```

```python
import functools
import math

import jax
import jax.numpy as jnp
from jax import lax
from jax.experimental import pallas as pl
from jax.experimental.pallas import tpu as pltpu
from jax.sharding import PartitionSpec as P

NFFT = 512
HALF = NFFT // 2
MESH = pl.DeviceIdType.MESH
F32 = jnp.float32
BF16 = jnp.bfloat16

ROWS = 16
PARTS = 1


def cosine(m):
    b = jnp.abs(m - 256) - 128
    x = b.astype(F32) * (2.0 * math.pi / NFFT)
    s = x * x
    p = jnp.full_like(x, 1.0 / math.factorial(13))
    for k in (11, 9, 7, 5, 3, 1):
        p = p * s + (-1.0 if k % 4 == 3 else 1.0) / math.factorial(k)
    return x * p


def iota(shape, dim):
    return lax.broadcasted_iota(jnp.int32, shape, dim)


def basis(freqs, first, n_tm):
    rows = 8 * n_tm
    row = iota((rows, freqs.shape[1]), 0)
    column = iota((rows, freqs.shape[1]), 1)
    wanted = 2 * lax.rem(first + row // 8, n_tm) + (row // 2) % 2
    freq = jnp.sum(jnp.where(column == wanted, freqs, 0).astype(F32), axis=1, keepdims=True)
    freq = freq.astype(jnp.int32)
    row = iota((rows, 1), 0)
    phase = freq * iota((rows, HALF), 1) + 128 * (row % 2)
    return cosine(phase & (NFFT - 1)), 1.0 - 2.0 * (freq & 1).astype(F32), (row // 4) % 2


def far_first(k, n):
    return n // 2 + jnp.where(k % 2 == 0, k // 2, -(k // 2))


def kernel(
    n_tm, n_space, lanes, scale,
    freq_hbm, x_hbm, out_ref,
    freq, x, even_w, left_w, right_w, swap,
    even, give_left, give_right, keep_left, keep_right, got_left, got_right, odd,
    recv, gram, mine, shares, total,
    freq_sem, x_sem, give_sem, got_sem, send_sem, recv_sem, space_send, space_recv,
):
    me = lax.axis_index("tm")
    spot = lax.axis_index("space")
    blocks = 2 * n_tm
    half = n_tm // 2
    width = 4 * lanes

    barrier = pltpu.get_barrier_semaphore()

    def load(part):
        columns = pl.ds(pl.multiple_of(part * width, width), width)
        return pltpu.make_async_copy(x_hbm.at[:, columns], x.at[part], x_sem.at[part])

    load_freq = pltpu.make_async_copy(freq_hbm, freq, freq_sem.at[0])
    load_freq.start()
    for part in range(PARTS):
        load(part).start()

    @pl.loop(1, n_tm, unroll=True)
    def _(k):
        other = lax.rem(me + far_first(k, n_tm), n_tm)
        pl.semaphore_signal(barrier, inc=1, device_id={"tm": other}, device_id_type=MESH)

    @pl.loop(1, n_space, unroll=True)
    def _(k):
        other = lax.rem(spot + far_first(k, n_space), n_space)
        pl.semaphore_signal(barrier, inc=1, device_id={"space": other}, device_id_type=MESH)


    window = 0.5 * cosine(iota((1, HALF), 1))
    rising, falling = 0.5 - window, 0.5 + window
    load_freq.wait()
    freqs = freq[...]
    wave, sign, which = basis(freqs, 0, n_tm)
    for h in range(2):
        kept = (which == h).astype(F32)
        even_w[h, :, :HALF] = (wave * rising * kept).astype(BF16)
        even_w[h, :, HALF:] = (wave * falling * (sign * kept)).astype(BF16)
    wave, sign, which = basis(freqs, me, n_tm)
    for h in range(2):
        left_w[h] = (wave * falling * (sign * (which == h).astype(F32))).astype(BF16)
    wave, sign, which = basis(freqs, me + 1, n_tm)
    for h in range(2):
        right_w[h] = (wave * rising * (which == h).astype(F32)).astype(BF16)

    side = ROWS * ROWS
    out_row, in_row = iota((side, side), 0), iota((side, side), 1)
    swap[...] = (in_row == (out_row % ROWS) * ROWS + out_row // ROWS).astype(F32).astype(BF16)

    def transform(part, weights, start, stop, owners=slice(None)):
        first, last, _ = owners.indices(n_tm)
        halves = []
        for pair in range(2):
            acc = None
            for h in range(2):
                columns = slice((2 * pair + h) * lanes, (2 * pair + h + 1) * lanes)
                term = jnp.dot(
                    weights[h, 8 * first : 8 * last],
                    x[part, start:stop, columns],
                    preferred_element_type=F32,
                )
                acc = term if acc is None else acc + term
            halves.append(acc.reshape(last - first, 8, lanes))
        return jnp.concatenate(halves, axis=1)

    def to_right(part):
        return pltpu.make_async_remote_copy(
            src_ref=give_right.at[part], dst_ref=got_left.at[part],
            send_sem=give_sem.at[0, part], recv_sem=got_sem.at[0, part],
            device_id={"tm": lax.rem(me + 1, n_tm)}, device_id_type=MESH,
        )

    def to_left(part):
        return pltpu.make_async_remote_copy(
            src_ref=give_left.at[part], dst_ref=got_right.at[part],
            send_sem=give_sem.at[1, part], recv_sem=got_sem.at[1, part],
            device_id={"tm": lax.rem(me + n_tm - 1, n_tm)}, device_id_type=MESH,
        )

    def post(part, tile, block, r):
        pltpu.make_async_remote_copy(
            src_ref=tile, dst_ref=recv.at[part, block],
            send_sem=send_sem.at[part], recv_sem=recv_sem.at[part],
            device_id={"tm": lax.rem(me + r, n_tm)}, device_id_type=MESH,
        ).start()

    def place(part, tile, block):
        pltpu.make_async_copy(tile, recv.at[part, block], recv_sem.at[part]).start()

    has_before, has_after = me > 0, me < n_tm - 1
    zeros = jnp.zeros((ROWS, lanes), BF16)
    for part in range(PARTS):
        recv[part, blocks - 1] = zeros

    after = 2 * me + 1
    before = 2 * me - 1

    @pl.loop(0, PARTS)
    def _(part):
        load(part).wait()
        partial = transform(part, left_w, 0, HALF)
        keep_left[part] = partial[:half]
        give_left[part] = partial[half:].astype(BF16)
        partial = transform(part, right_w, HALF, NFFT)
        give_right[part] = partial[:half].astype(BF16)
        keep_right[part] = partial[half:]

        @pl.when(part == 0)
        def _():
            pl.semaphore_wait(barrier, n_tm + n_space - 2)


        @pl.when(has_after)
        def _():
            to_right(part).start()

        @pl.when(has_before)
        def _():
            to_left(part).start()

        for first in range(0, n_tm, half):
            owners = slice(first, first + half)
            even[part, owners] = transform(part, even_w, 0, NFFT, owners).astype(BF16)

            @pl.loop(first, first + half)
            def _(k):
                @pl.when(k == me)
                def _():
                    place(part, even.at[part, k], 2 * me)

                @pl.when(k != me)
                def _():
                    post(part, even.at[part, k], 2 * me, lax.rem(k + n_tm - me, n_tm))

    @pl.loop(0, PARTS)
    def _(part):
        @pl.when(has_before)
        def _():
            to_right(part).wait_recv()
            odd[part, :half] = (keep_left[part] + got_left[part].astype(F32)).astype(BF16)
            place(part, odd.at[part, 0], before)

        @pl.when(has_after)
        def _():
            to_left(part).wait_recv()
            summed = (keep_right[part] + got_right[part].astype(F32)).astype(BF16)
            odd[part, half + 1 :] = summed[: half - 1]
            odd[part, half] = summed[half - 1]
            place(part, odd.at[part, half], after)

        @pl.loop(0, n_tm)
        def _(k):
            r = lax.rem(k + n_tm - me, n_tm)

            @pl.when((r > 0) & (r < half) & has_before)
            def _():
                post(part, odd.at[part, r], before, r)

            @pl.when((r > half) & has_after)
            def _():
                post(part, odd.at[part, r], after, r)

    gram[...] = jnp.zeros_like(gram)

    @pl.loop(0, PARTS)
    def _(part):
        arrived = recv.at[part, pl.ds(0, blocks - 1)]
        pltpu.make_async_copy(arrived, arrived, recv_sem.at[part]).wait()
        groups = []
        for g in range(blocks // ROWS):
            tiles = recv[part, g * ROWS : (g + 1) * ROWS].reshape(side, lanes)
            groups.append(jnp.dot(swap[...], tiles, preferred_element_type=F32).astype(BF16))
        for f in range(2):
            acc = gram[f]
            for q in range(4):
                rows = [
                    group[(4 * q + 2 * f + c) * ROWS : (4 * q + 2 * f + c + 1) * ROWS]
                    for c in range(2)
                    for group in groups
                ]
                rows = jnp.concatenate(rows, axis=0)
                acc = acc + lax.dot_general(
                    rows, rows, (((1,), (1,)), ((), ())), preferred_element_type=F32
                )
            gram[f] = acc

    for f in range(2):
        both = gram[f]
        top, bottom = both[:blocks], both[blocks:]
        real_side = iota(top.shape, 1) < blocks
        mine[f * blocks : (f + 1) * blocks, :] = jnp.where(real_side, top, -top) + jnp.concatenate(
            [bottom[:, blocks:], bottom[:, :blocks]], axis=1
        )

    share = 2 * blocks // n_space

    def rows_of(spot):
        return pl.ds(pl.multiple_of(spot * share, share), share)

    @pl.loop(1, n_space)
    def _(k):
        other = lax.rem(spot + far_first(k, n_space), n_space)
        pltpu.make_async_remote_copy(
            src_ref=mine.at[rows_of(other)], dst_ref=shares.at[spot],
            send_sem=space_send.at[0], recv_sem=space_recv.at[0],
            device_id={"space": other}, device_id_type=MESH,
        ).start()

    shares[spot] = mine[rows_of(spot), :]
    others = shares.at[pl.ds(0, n_space - 1)]
    pltpu.make_async_copy(others, others, space_recv.at[0]).wait()
    total[rows_of(spot), :] = jnp.sum(shares[...], axis=0) * scale

    @pl.loop(1, n_space)
    def _(k):
        other = lax.rem(spot + far_first(k, n_space), n_space)
        pltpu.make_async_remote_copy(
            src_ref=total.at[rows_of(spot)], dst_ref=total.at[rows_of(spot)],
            send_sem=space_send.at[1], recv_sem=space_recv.at[1],
            device_id={"space": other}, device_id_type=MESH,
        ).start()

    for part in range(PARTS):
        sent = recv.at[part, pl.ds(0, n_tm - 1)]
        pltpu.make_async_copy(sent, sent, send_sem.at[part]).wait()
        sent = recv.at[part, pl.ds(0, half - 1)]

        @pl.when(has_after)
        def _():
            to_right(part).wait_send()
            pltpu.make_async_copy(sent, sent, send_sem.at[part]).wait()

        @pl.when(has_before)
        def _():
            to_left(part).wait_send()
            pltpu.make_async_copy(sent, sent, send_sem.at[part]).wait()

    pltpu.make_async_copy(others, others, space_send.at[0]).wait()
    pltpu.make_async_copy(others, others, space_recv.at[1]).wait()
    for f in range(2):
        rows = total[f * blocks : (f + 1) * blocks, :]
        out_ref[f, :, 0, :] = rows[: blocks - 1, : blocks - 1]
        out_ref[f, :, 1, :] = rows[: blocks - 1, blocks : 2 * blocks - 1]
    pltpu.make_async_copy(others, others, space_send.at[1]).wait()


def local(snapshots, freq_ids):
    n_tm, n_space = lax.axis_size("tm"), lax.axis_size("space")
    points = snapshots.shape[1]
    lanes = points // (4 * PARTS)
    blocks, half, rows = 2 * n_tm, n_tm // 2, 8 * n_tm
    dma = pltpu.SemaphoreType.DMA
    out = pl.pallas_call(
        functools.partial(kernel, n_tm, n_space, lanes, 1.0 / (NFFT * points * n_space)),
        out_shape=jax.ShapeDtypeStruct((2, blocks - 1, 2, blocks - 1), F32),
        in_specs=[
            pl.BlockSpec(memory_space=pl.ANY),
            pl.BlockSpec(memory_space=pl.ANY),
        ],
        out_specs=pl.BlockSpec(memory_space=pltpu.VMEM),
        scratch_shapes=[
            pltpu.VMEM((1, freq_ids.shape[0]), jnp.int32),
            pltpu.VMEM((PARTS, NFFT, 4 * lanes), BF16),
            pltpu.VMEM((2, rows, NFFT), BF16),
            pltpu.VMEM((2, rows, HALF), BF16),
            pltpu.VMEM((2, rows, HALF), BF16),
            pltpu.VMEM((ROWS * ROWS, ROWS * ROWS), BF16),
            pltpu.VMEM((PARTS, n_tm, ROWS, lanes), BF16),
            pltpu.VMEM((PARTS, half, ROWS, lanes), BF16),
            pltpu.VMEM((PARTS, half, ROWS, lanes), BF16),
            pltpu.VMEM((PARTS, half, ROWS, lanes), F32),
            pltpu.VMEM((PARTS, half, ROWS, lanes), F32),
            pltpu.VMEM((PARTS, half, ROWS, lanes), BF16),
            pltpu.VMEM((PARTS, half, ROWS, lanes), BF16),
            pltpu.VMEM((PARTS, n_tm, ROWS, lanes), BF16),
            pltpu.VMEM((PARTS, blocks, ROWS, lanes), BF16),
            pltpu.VMEM((2, 2 * blocks, 2 * blocks), F32),
            pltpu.VMEM((2 * blocks, 2 * blocks), F32),
            pltpu.VMEM((n_space, 2 * blocks // n_space, 2 * blocks), F32),
            pltpu.VMEM((2 * blocks, 2 * blocks), F32),
            dma((1,)),
            dma((PARTS,)),
            dma((2, PARTS)),
            dma((2, PARTS)),
            dma((PARTS,)),
            dma((PARTS,)),
            dma((2,)),
            dma((2,)),
        ],
        compiler_params=pltpu.CompilerParams(
            collective_id=0, has_side_effects=True, vmem_limit_bytes=48 * 2**20
        ),
        name="spod",
    )(
        pltpu.with_memory_space_constraint(freq_ids.reshape(1, -1), pltpu.HBM),
        pltpu.with_memory_space_constraint(snapshots, pltpu.HBM),
    )
    return out.transpose(0, 2, 1, 3)


def solution(mesh):
    return jax.shard_map(
        local,
        mesh=mesh,
        in_specs=(P("tm", "space"), P()),
        out_specs=P("tm", None, None, None),
        check_vma=False,
    )
```

```python
import functools
import math

import jax
import jax.numpy as jnp
from jax import lax
from jax.experimental import pallas as pl
from jax.experimental.pallas import tpu as pltpu
from jax.sharding import PartitionSpec as P

NFFT = 512
HALF = NFFT // 2
MESH = pl.DeviceIdType.MESH
F32 = jnp.float32
BF16 = jnp.bfloat16

ROWS = 16
PARTS = 1


def cosine(m):
    b = jnp.abs(m - 256) - 128
    x = b.astype(F32) * (2.0 * math.pi / NFFT)
    s = x * x
    p = jnp.full_like(x, 1.0 / math.factorial(13))
    for k in (11, 9, 7, 5, 3, 1):
        p = p * s + (-1.0 if k % 4 == 3 else 1.0) / math.factorial(k)
    return x * p


def iota(shape, dim):
    return lax.broadcasted_iota(jnp.int32, shape, dim)


def basis(freqs, first, n_tm):
    rows = 8 * n_tm
    row = iota((rows, freqs.shape[1]), 0)
    column = iota((rows, freqs.shape[1]), 1)
    wanted = 2 * lax.rem(first + row // 8, n_tm) + (row // 2) % 2
    freq = jnp.sum(jnp.where(column == wanted, freqs, 0).astype(F32), axis=1, keepdims=True)
    freq = freq.astype(jnp.int32)
    row = iota((rows, 1), 0)
    phase = freq * iota((rows, HALF), 1) + 128 * (row % 2)
    return cosine(phase & (NFFT - 1)), 1.0 - 2.0 * (freq & 1).astype(F32), (row // 4) % 2


def far_first(k, n):
    return n // 2 + jnp.where(k % 2 == 0, k // 2, -(k // 2))


def kernel(
    n_tm, n_space, lanes, scale,
    freq_hbm, x_hbm, out_ref,
    freq, x, even_w, left_w, right_w, swap,
    even, give_left, give_right, keep_left, keep_right, got_left, got_right, odd,
    recv, gram, mine, shares, total,
    freq_sem, x_sem, give_sem, got_sem, send_sem, recv_sem, space_send, space_recv,
):
    me = lax.axis_index("tm")
    spot = lax.axis_index("space")
    blocks = 2 * n_tm
    half = n_tm // 2
    width = 4 * lanes

    barrier = pltpu.get_barrier_semaphore()

    def load(part):
        columns = pl.ds(pl.multiple_of(part * width, width), width)
        return pltpu.make_async_copy(x_hbm.at[:, columns], x.at[part], x_sem.at[part])

    load_freq = pltpu.make_async_copy(freq_hbm, freq, freq_sem.at[0])
    load_freq.start()
    for part in range(PARTS):
        load(part).start()

    @pl.loop(1, n_tm, unroll=True)
    def _(k):
        other = lax.rem(me + far_first(k, n_tm), n_tm)
        pl.semaphore_signal(barrier, inc=1, device_id={"tm": other}, device_id_type=MESH)

    @pl.loop(1, n_space, unroll=True)
    def _(k):
        other = lax.rem(spot + far_first(k, n_space), n_space)
        pl.semaphore_signal(barrier, inc=1, device_id={"space": other}, device_id_type=MESH)


    window = 0.5 * cosine(iota((1, HALF), 1))
    rising, falling = 0.5 - window, 0.5 + window
    load_freq.wait()
    freqs = freq[...]
    wave, sign, which = basis(freqs, 0, n_tm)
    for h in range(2):
        kept = (which == h).astype(F32)
        even_w[h, :, :HALF] = (wave * rising * kept).astype(BF16)
        even_w[h, :, HALF:] = (wave * falling * (sign * kept)).astype(BF16)
    wave, sign, which = basis(freqs, me, n_tm)
    for h in range(2):
        left_w[h] = (wave * falling * (sign * (which == h).astype(F32))).astype(BF16)
    wave, sign, which = basis(freqs, me + 1, n_tm)
    for h in range(2):
        right_w[h] = (wave * rising * (which == h).astype(F32)).astype(BF16)

    side = ROWS * ROWS
    out_row, in_row = iota((side, side), 0), iota((side, side), 1)
    swap[...] = (in_row == (out_row % ROWS) * ROWS + out_row // ROWS).astype(F32).astype(BF16)

    def transform(part, weights, start, stop, owners=slice(None)):
        first, last, _ = owners.indices(n_tm)
        halves = []
        for pair in range(2):
            acc = None
            for h in range(2):
                columns = slice((2 * pair + h) * lanes, (2 * pair + h + 1) * lanes)
                term = jnp.dot(
                    weights[h, 8 * first : 8 * last],
                    x[part, start:stop, columns],
                    preferred_element_type=F32,
                )
                acc = term if acc is None else acc + term
            halves.append(acc.reshape(last - first, 8, lanes))
        return jnp.concatenate(halves, axis=1)

    def to_right(part):
        return pltpu.make_async_remote_copy(
            src_ref=give_right.at[part], dst_ref=got_left.at[part],
            send_sem=give_sem.at[0, part], recv_sem=got_sem.at[0, part],
            device_id={"tm": lax.rem(me + 1, n_tm)}, device_id_type=MESH,
        )

    def to_left(part):
        return pltpu.make_async_remote_copy(
            src_ref=give_left.at[part], dst_ref=got_right.at[part],
            send_sem=give_sem.at[1, part], recv_sem=got_sem.at[1, part],
            device_id={"tm": lax.rem(me + n_tm - 1, n_tm)}, device_id_type=MESH,
        )

    def post(part, tile, block, r):
        pltpu.make_async_remote_copy(
            src_ref=tile, dst_ref=recv.at[part, block],
            send_sem=send_sem.at[part], recv_sem=recv_sem.at[part],
            device_id={"tm": lax.rem(me + r, n_tm)}, device_id_type=MESH,
        ).start()

    def place(part, tile, block):
        pltpu.make_async_copy(tile, recv.at[part, block], recv_sem.at[part]).start()

    has_before, has_after = me > 0, me < n_tm - 1
    zeros = jnp.zeros((ROWS, lanes), BF16)
    for part in range(PARTS):
        recv[part, blocks - 1] = zeros

    after = 2 * me + 1
    before = 2 * me - 1

    @pl.loop(0, PARTS)
    def _(part):
        load(part).wait()
        partial = transform(part, left_w, 0, HALF)
        keep_left[part] = partial[:half]
        give_left[part] = partial[half:].astype(BF16)
        partial = transform(part, right_w, HALF, NFFT)
        give_right[part] = partial[:half].astype(BF16)
        keep_right[part] = partial[half:]

        @pl.when(part == 0)
        def _():
            pl.semaphore_wait(barrier, n_tm + n_space - 2)


        @pl.when(has_after)
        def _():
            to_right(part).start()

        @pl.when(has_before)
        def _():
            to_left(part).start()

        for first in range(0, n_tm, half):
            owners = slice(first, first + half)
            even[part, owners] = transform(part, even_w, 0, NFFT, owners).astype(BF16)

            @pl.loop(first, first + half)
            def _(k):
                @pl.when(k == me)
                def _():
                    place(part, even.at[part, k], 2 * me)

                @pl.when(k != me)
                def _():
                    post(part, even.at[part, k], 2 * me, lax.rem(k + n_tm - me, n_tm))

    @pl.loop(0, PARTS)
    def _(part):
        @pl.when(has_before)
        def _():
            to_right(part).wait_recv()
            odd[part, :half] = (keep_left[part] + got_left[part].astype(F32)).astype(BF16)
            place(part, odd.at[part, 0], before)

        @pl.when(has_after)
        def _():
            to_left(part).wait_recv()
            summed = (keep_right[part] + got_right[part].astype(F32)).astype(BF16)
            odd[part, half + 1 :] = summed[: half - 1]
            odd[part, half] = summed[half - 1]
            place(part, odd.at[part, half], after)

        @pl.loop(0, n_tm)
        def _(k):
            r = lax.rem(k + n_tm - me, n_tm)

            @pl.when((r > 0) & (r < half) & has_before)
            def _():
                post(part, odd.at[part, r], before, r)

            @pl.when((r > half) & has_after)
            def _():
                post(part, odd.at[part, r], after, r)

    gram[...] = jnp.zeros_like(gram)

    @pl.loop(0, PARTS)
    def _(part):
        arrived = recv.at[part, pl.ds(0, blocks - 1)]
        pltpu.make_async_copy(arrived, arrived, recv_sem.at[part]).wait()
        groups = []
        for g in range(blocks // ROWS):
            tiles = recv[part, g * ROWS : (g + 1) * ROWS].reshape(side, lanes)
            groups.append(jnp.dot(swap[...], tiles, preferred_element_type=F32).astype(BF16))
        for f in range(2):
            acc = gram[f]
            for q in range(4):
                rows = [
                    group[(4 * q + 2 * f + c) * ROWS : (4 * q + 2 * f + c + 1) * ROWS]
                    for c in range(2)
                    for group in groups
                ]
                rows = jnp.concatenate(rows, axis=0)
                acc = acc + lax.dot_general(
                    rows, rows, (((1,), (1,)), ((), ())), preferred_element_type=F32
                )
            gram[f] = acc

    for f in range(2):
        both = gram[f]
        top, bottom = both[:blocks], both[blocks:]
        real_side = iota(top.shape, 1) < blocks
        mine[f * blocks : (f + 1) * blocks, :] = jnp.where(real_side, top, -top) + jnp.concatenate(
            [bottom[:, blocks:], bottom[:, :blocks]], axis=1
        )

    share = 2 * blocks // n_space

    def rows_of(spot):
        return pl.ds(pl.multiple_of(spot * share, share), share)

    @pl.loop(1, n_space, unroll=True)
    def _(k):
        other = lax.rem(spot + far_first(k, n_space), n_space)
        pltpu.make_async_remote_copy(
            src_ref=mine.at[rows_of(other)], dst_ref=shares.at[spot],
            send_sem=space_send.at[0], recv_sem=space_recv.at[0],
            device_id={"space": other}, device_id_type=MESH,
        ).start()

    shares[spot] = mine[rows_of(spot), :]
    others = shares.at[pl.ds(0, n_space - 1)]
    pltpu.make_async_copy(others, others, space_recv.at[0]).wait()
    total[rows_of(spot), :] = jnp.sum(shares[...], axis=0) * scale

    @pl.loop(1, n_space, unroll=True)
    def _(k):
        other = lax.rem(spot + far_first(k, n_space), n_space)
        pltpu.make_async_remote_copy(
            src_ref=total.at[rows_of(spot)], dst_ref=total.at[rows_of(spot)],
            send_sem=space_send.at[1], recv_sem=space_recv.at[1],
            device_id={"space": other}, device_id_type=MESH,
        ).start()

    for part in range(PARTS):
        sent = recv.at[part, pl.ds(0, n_tm - 1)]
        pltpu.make_async_copy(sent, sent, send_sem.at[part]).wait()
        sent = recv.at[part, pl.ds(0, half - 1)]

        @pl.when(has_after)
        def _():
            to_right(part).wait_send()
            pltpu.make_async_copy(sent, sent, send_sem.at[part]).wait()

        @pl.when(has_before)
        def _():
            to_left(part).wait_send()
            pltpu.make_async_copy(sent, sent, send_sem.at[part]).wait()

    pltpu.make_async_copy(others, others, space_send.at[0]).wait()
    pltpu.make_async_copy(others, others, space_recv.at[1]).wait()
    for f in range(2):
        rows = total[f * blocks : (f + 1) * blocks, :]
        out_ref[f, :, 0, :] = rows[: blocks - 1, : blocks - 1]
        out_ref[f, :, 1, :] = rows[: blocks - 1, blocks : 2 * blocks - 1]
    pltpu.make_async_copy(others, others, space_send.at[1]).wait()


def local(snapshots, freq_ids):
    n_tm, n_space = lax.axis_size("tm"), lax.axis_size("space")
    points = snapshots.shape[1]
    lanes = points // (4 * PARTS)
    blocks, half, rows = 2 * n_tm, n_tm // 2, 8 * n_tm
    dma = pltpu.SemaphoreType.DMA
    out = pl.pallas_call(
        functools.partial(kernel, n_tm, n_space, lanes, 1.0 / (NFFT * points * n_space)),
        out_shape=jax.ShapeDtypeStruct((2, blocks - 1, 2, blocks - 1), F32),
        in_specs=[
            pl.BlockSpec(memory_space=pl.ANY),
            pl.BlockSpec(memory_space=pl.ANY),
        ],
        out_specs=pl.BlockSpec(memory_space=pltpu.VMEM),
        scratch_shapes=[
            pltpu.VMEM((1, freq_ids.shape[0]), jnp.int32),
            pltpu.VMEM((PARTS, NFFT, 4 * lanes), BF16),
            pltpu.VMEM((2, rows, NFFT), BF16),
            pltpu.VMEM((2, rows, HALF), BF16),
            pltpu.VMEM((2, rows, HALF), BF16),
            pltpu.VMEM((ROWS * ROWS, ROWS * ROWS), BF16),
            pltpu.VMEM((PARTS, n_tm, ROWS, lanes), BF16),
            pltpu.VMEM((PARTS, half, ROWS, lanes), BF16),
            pltpu.VMEM((PARTS, half, ROWS, lanes), BF16),
            pltpu.VMEM((PARTS, half, ROWS, lanes), F32),
            pltpu.VMEM((PARTS, half, ROWS, lanes), F32),
            pltpu.VMEM((PARTS, half, ROWS, lanes), BF16),
            pltpu.VMEM((PARTS, half, ROWS, lanes), BF16),
            pltpu.VMEM((PARTS, n_tm, ROWS, lanes), BF16),
            pltpu.VMEM((PARTS, blocks, ROWS, lanes), BF16),
            pltpu.VMEM((2, 2 * blocks, 2 * blocks), F32),
            pltpu.VMEM((2 * blocks, 2 * blocks), F32),
            pltpu.VMEM((n_space, 2 * blocks // n_space, 2 * blocks), F32),
            pltpu.VMEM((2 * blocks, 2 * blocks), F32),
            dma((1,)),
            dma((PARTS,)),
            dma((2, PARTS)),
            dma((2, PARTS)),
            dma((PARTS,)),
            dma((PARTS,)),
            dma((2,)),
            dma((2,)),
        ],
        compiler_params=pltpu.CompilerParams(
            collective_id=0, has_side_effects=True, vmem_limit_bytes=48 * 2**20
        ),
        name="spod",
    )(
        pltpu.with_memory_space_constraint(freq_ids.reshape(1, -1), pltpu.HBM),
        pltpu.with_memory_space_constraint(snapshots, pltpu.HBM),
    )
    return out.transpose(0, 2, 1, 3)


def solution(mesh):
    return jax.shard_map(
        local,
        mesh=mesh,
        in_specs=(P("tm", "space"), P()),
        out_specs=P("tm", None, None, None),
        check_vma=False,
    )
```
